32 devices in a mesh: gx: 4 (over z), gy: 8 (over y, x, core).
Axes of the slice: x: 2, y: 2, z: 4, core: 2. Of those that a mesh axis runs over, the one named last changes fastest.
Arguments:
- state: float32 [10, 32, 32768], P(None, None, ('gx', 'gy'))
- kdist: bfloat16 [224, 32], replicated, may hold values from 9.9658966e-05 to 0.049804688
- rayleigh: float32 [224], replicated, may hold values from 0.002 to 0.05
- solar: float32 [224], replicated, may hold values from 0.002 to 0.01
- span_map: int32 [32768], P(('gx', 'gy')), may hold values from 0 to 32767, as said below
- cos_zenith: float32 [32768], P(('gx', 'gy')), may hold values from -1 to 1, as said below
- day_flag: int32 [32768], P(('gx', 'gy')), may hold values from 0 to 1, as said below
- albedo: float32 [32768], P(('gx', 'gy')), may hold values from 0.05 to 0.8
Outputs:
- heating: float32 [32, 32768], P(None, ('gx', 'gy'))
- surface: float32 [3, 32768], P(None, ('gx', 'gy'))
The draws below stay inside these ranges and needn't reach their ends.
Inputs may be any that keep to these rules, and one draw needn't show every extreme that they name: span_map is a permutation of the 32768 columns; a column held by device s (index in gx+gy order) goes to a column p with (p % 1024) // 32 == s, and each device's columns reach every device equally often. `cos_zenith`: column j of device d (index in gx+gy order) and column 1023 - j of the device whose index differs from d by 16 are antipodes: their values are opposite, of magnitude 0.05 or more. `day_flag`: 1 exactly where cos_zenith > 0.
All inputs are finite; a program needn't handle non-finite values.
Results may differ from the reference program's by a relative error of at most 0.00069.
Values sent between devices are 32-bit elements; how exact they have to be, the bound alone decides.
A program may use at most 64 MiB of HBM per device.

```python
import math
import jax
import jax.numpy as jnp
from jax import lax

G = 224
NGAS = 8
NLEV = 32
COLS_DEV = 1024
NPRED = 32
NCOL = 32768
N_GX = 4
N_GY = 8


def antipode_signs(key):
    devices = N_GX * N_GY
    lower_count = devices // 2
    initial_height_index, second = jax.random.split(jax.random.fold_in(key, 7))
    levels = jax.random.randint(initial_height_index, (lower_count, 1), 1, 8)
    draws = jax.random.randint(second, (lower_count, COLS_DEV), 0, 8)
    lower_half = jnp.where(draws < levels, 1, -1).astype(jnp.int32)
    upper_half = -lower_half[:, ::-1]
    return jnp.concatenate([lower_half, upper_half], 0).reshape(-1)


def draw_day_flag(key, part):
    signs = antipode_signs(key)
    return jnp.where(signs > 0, 1, 0).astype(jnp.int32)


def draw_cos_zenith(key, part):
    signs = antipode_signs(key).astype(jnp.float32)
    devices = N_GX * N_GY
    uniform_part = jax.random.uniform(jax.random.fold_in(key, 9), (devices // 2, COLS_DEV), jnp.float32)
    magnitude = 0.05 + 0.95 * uniform_part
    full = jnp.concatenate([magnitude, magnitude[:, ::-1]], 0).reshape(-1)
    return (signs * full).astype(jnp.float32)


def draw_span_map(key, part):
    devices = N_GX * N_GY
    per_peer = COLS_DEV // devices
    keys = jax.random.split(jax.random.fold_in(key, 5), devices)
    orders = jax.vmap(lambda single: jax.random.permutation(single, COLS_DEV))(keys).astype(jnp.int32)
    source = jnp.arange(devices, dtype=jnp.int32)[:, None]
    target = orders // per_peer * COLS_DEV + source * per_peer + orders % per_peer
    return target.reshape(-1).astype(jnp.int32)


def draw_state(key, part):
    initial_height_index, second, third = jax.random.split(jax.random.fold_in(key, 11), 3)
    dimension_tuple = (NLEV, NCOL)
    kelvin_profile = jax.random.uniform(initial_height_index, dimension_tuple, jnp.float32, 190.0, 310.0)
    slab_weight_per_area = jnp.exp(jax.random.uniform(second, dimension_tuple, jnp.float32, -1.2, 1.1))
    absorber_columns = jnp.exp(jax.random.uniform(third, (NGAS, NLEV, NCOL), jnp.float32, -4.6, 0.0))
    return jnp.concatenate([kelvin_profile[None], slab_weight_per_area[None], absorber_columns], 0).astype(jnp.float32)


def block_scale(key, extent, cuts, least, high):
    factor_of, own = 1.0, jax.random.fold_in(key, 6)
    for dim, shards_of in cuts:
        steps = jnp.exp(jax.random.uniform(jax.random.fold_in(own, dim), (shards_of,), jnp.float32, least / len(cuts), high / len(cuts)))
        factor_of = factor_of * jnp.repeat(steps, extent[dim] // shards_of).reshape([-1 if axis == dim else 1 for axis in range(len(extent))])
    return factor_of


def setup_inputs(seed: int = 0) -> dict:
    key_of = jax.random.split(jax.random.key(seed), 9)
    return {
        "state": draw_state(jax.random.fold_in(key_of[8], 71), 0),
        "kdist": jnp.clip(jnp.exp(jax.random.uniform(key_of[1], (G, NPRED), jnp.float32, math.log(9.965896606445312e-05), math.log(0.049804688))), 9.965896606445312e-05, 0.049804688).astype(jnp.bfloat16),
        "rayleigh": jnp.clip(jnp.exp(jax.random.uniform(key_of[2], (G,), jnp.float32, math.log(0.002), math.log(0.05))), 0.002, 0.05),
        "solar": jnp.clip(jnp.exp(jax.random.uniform(key_of[3], (G,), jnp.float32, math.log(0.002), math.log(0.01))), 0.002, 0.01),
        "span_map": draw_span_map(jax.random.fold_in(key_of[8], 71), 0),
        "cos_zenith": draw_cos_zenith(jax.random.fold_in(key_of[8], 71), 0),
        "day_flag": draw_day_flag(jax.random.fold_in(key_of[8], 71), 0),
        "albedo": jnp.clip(0.05 + 0.75 * jax.random.uniform(key_of[7], (NCOL,), jnp.float32) ** block_scale(key_of[7], (NCOL,), ((0, 32),), -0.2, 0.2), 0.05, 0.8),
    }


diffusivity = 1.66
heat_factor = 8.0


def upward(carried, layer):
    albedo_below, source_below = carried
    reflect, transmit, direct_src = layer
    divisor = 1.0 - reflect * albedo_below
    albedo_top = reflect + transmit * transmit * albedo_below / divisor
    source_top = direct_src + transmit * (source_below + albedo_below * direct_src) / divisor
    return (albedo_top, source_top), (albedo_below, source_below)


def downward(diffuse, layer):
    reflect, transmit, direct_src, albedo_below, source_below = layer
    lower_down = (transmit * diffuse + direct_src + reflect * source_below) / (1.0 - reflect * albedo_below)
    lower_up = albedo_below * lower_down + source_below
    return lower_down, (lower_down, lower_up)


def column_physics(quantity_bundle, cosine, albedo, kdist, rayleigh, solar):
    levels = quantity_bundle.shape[1]
    columns = quantity_bundle.shape[2]
    kelvin_profile = quantity_bundle[0] / 250.0
    slab_weight_per_area = quantity_bundle[1]
    expansion_modes = jnp.stack([jnp.ones_like(kelvin_profile), kelvin_profile, kelvin_profile * kelvin_profile, 1.0 / kelvin_profile])
    predictors = (quantity_bundle[2:, None] * expansion_modes[None] * slab_weight_per_area).astype(jnp.bfloat16)
    predictors = predictors.reshape(-1, levels, columns)
    block_width = math.gcd(kdist.shape[0], 32)
    blocks = kdist.shape[0] // block_width

    def one_block(block_index):
        start = block_index * block_width
        k_rows = lax.dynamic_slice_in_dim(kdist, start, block_width, 0)
        ray_rows = lax.dynamic_slice_in_dim(rayleigh, start, block_width, 0)
        sun_rows = lax.dynamic_slice_in_dim(solar, start, block_width, 0)
        tau_gas = jnp.einsum("gp,plc->lgc", k_rows.astype(jnp.float32), predictors.astype(jnp.float32), precision=lax.Precision.HIGHEST)
        tau_ray = ray_rows[None, :, None] * slab_weight_per_area[:, None, :]
        optical = tau_gas + tau_ray
        albedo_single = tau_ray / optical
        extinct = jnp.exp(-diffusivity * optical)
        reflect = 0.5 * albedo_single * (1.0 - extinct)
        transmit = extinct + reflect
        cumulative = jnp.cumsum(optical, axis=0)
        above = cumulative - optical
        direct_top = sun_rows[None, :, None] * cosine * jnp.exp(-above / cosine)
        direct_bottom = sun_rows[:, None] * cosine * jnp.exp(-cumulative[-1] / cosine)
        direct_src = 0.5 * albedo_single * (1.0 - jnp.exp(-optical / cosine)) * direct_top
        start_albedo = jnp.broadcast_to(albedo, direct_bottom.shape)
        (albedo_end, source_top), (albedo_below, source_below) = lax.scan(upward, (start_albedo, albedo * direct_bottom), (reflect, transmit, direct_src), reverse=True)
        zeros = jnp.zeros_like(direct_bottom)
        final_down, (lower_down, lower_up) = lax.scan(downward, zeros, (reflect, transmit, direct_src, albedo_below, source_below))
        direct_all = jnp.concatenate([direct_top, direct_bottom[None]], 0)
        down_all = jnp.concatenate([zeros[None], lower_down], 0)
        up_all = jnp.concatenate([source_top[None], lower_up], 0)
        net = jnp.sum(direct_all + down_all - up_all, axis=1)
        surface = jnp.stack([jnp.sum(direct_bottom, 0), jnp.sum(final_down, 0), jnp.sum(source_top, 0)])
        return net, surface

    nets, surfaces = lax.map(one_block, jnp.arange(blocks, dtype=jnp.int32))
    net = jnp.sum(nets, 0)
    heat_rate = heat_factor * (net[:-1] - net[1:]) / slab_weight_per_area
    return heat_rate, jnp.sum(surfaces, 0)


def reference(state, kdist, rayleigh, solar, span_map, cos_zenith, day_flag, albedo):
    spanned = jnp.zeros_like(state).at[:, :, span_map].set(state)
    groups = spanned.shape[-1] // COLS_DEV
    daylit = day_flag.astype(jnp.float32)
    cosine_all = jnp.where(day_flag == 1, cos_zenith, jnp.float32(1.0))

    def one_group(group_index):
        start = group_index * COLS_DEV
        quantity_bundle = lax.dynamic_slice_in_dim(spanned, start, COLS_DEV, 2)
        cosine = lax.dynamic_slice_in_dim(cosine_all, start, COLS_DEV, 0)
        ground = lax.dynamic_slice_in_dim(albedo, start, COLS_DEV, 0)
        mask = lax.dynamic_slice_in_dim(daylit, start, COLS_DEV, 0)
        heat_rate, surface = column_physics(quantity_bundle, cosine, ground, kdist, rayleigh, solar)
        return heat_rate * mask, surface * mask

    heat_rate, surface = lax.map(one_group, jnp.arange(groups, dtype=jnp.int32))
    heat_span = jnp.moveaxis(heat_rate, 0, 1).reshape(NLEV, -1)
    surface = jnp.moveaxis(surface, 0, 1).reshape(3, -1)
    heating = jnp.take(heat_span, span_map, axis=1)
    return heating, surface
```

```python
import functools
import math

import jax
import jax.numpy as jnp
from jax import lax
from jax.experimental import pallas as pl
from jax.experimental.pallas import tpu as pltpu
from jax.sharding import PartitionSpec as P

diffusivity = 1.66
heat_factor = 8.0
LANES = 128
SUBS = 8
PACKS = (1, 2, 4)
LOG2E = math.log2(math.e)
f32 = jnp.float32
bf16 = jnp.bfloat16


def pieces(x, count):
    out = []
    for _ in range(count):
        part = x.astype(bf16)
        out.append(part)
        x = x - part.astype(f32)
    return out


def dot_t(a, b):
    return lax.dot_general(a, b, (((1,), (1,)), ((), ())), preferred_element_type=f32)


def dot(a, b):
    return jnp.dot(a, b, preferred_element_type=f32)


def physics_kernel(
    per_peer, state_ref, rows_ref, span_ref, kdist_ref, gray_ref, gsol_ref,
    heat_ref, surf_ref,
    tab_ref, wide_ref, ray_ref, sol_ref,
    pm_ref, ca_ref, kk_ref, comp_ref, mc_ref, rhs_ref, mt_ref, ct_ref,
    tau_ref, q_ref, v_ref, e_ref, a_ref, s_ref, net_ref,
):
    levels, cols = heat_ref.shape
    npred = 4 * (state_ref.shape[0] - 2)
    section = rhs_ref.shape[0] // PACKS[-1]
    g = kdist_ref.shape[1]
    gb = g // PACKS[-1]
    c_diff = -diffusivity * LOG2E
    lane_rows = cols // LANES
    lane = lax.broadcasted_iota(jnp.int32, (1, LANES), 1)

    tab_ref[...] = jnp.zeros_like(tab_ref)
    high, low = pieces(kdist_ref[...].astype(f32) * c_diff, 2)
    tab_ref[0:npred, 0:g] = high.astype(f32)
    tab_ref[npred:2 * npred, 0:g] = low.astype(f32)
    gray = gray_ref[...]
    rh, rm, rl = [part.astype(f32) for part in pieces(gray * c_diff, 3)]
    sub16g = lax.broadcasted_iota(jnp.int32, (16, g), 0)
    tail16 = jnp.zeros((16, g), f32)
    for i, row in enumerate((rh, rh, rm, rh, rl, rm, gray * (0.5 * c_diff), gsol_ref[...])):
        tail16 = jnp.where(sub16g == i, row, tail16)
    tab_ref[2 * npred:2 * npred + 16, 0:g] = tail16
    turned = jnp.transpose(tab_ref[...])
    wide_ref[...] = turned
    for col, ref in ((2 * npred + 6, ray_ref), (2 * npred + 7, sol_ref)):
        spread = jnp.broadcast_to(turned[:g, col:col + 1], (g, LANES))
        at = 0
        for r in PACKS:
            rows = g // r
            value = spread[:rows]
            for q in range(1, r):
                value = jnp.where(lane >= q * (LANES // r), spread[q * rows:(q + 1) * rows], value)
            ref[at:at + rows, :] = value
            at += rows

    t = state_ref[0] / 250.0
    m_all = state_ref[1]
    basis = (None, t, t * t, 1.0 / t)
    for i in range(npred // 4):
        gas = state_ref[2 + i]
        for b in range(4):
            value = gas if b == 0 else gas * basis[b]
            pm_ref[pl.ds((4 * i + b) * levels, levels), :] = (value * m_all).astype(bf16)
    for i, part in enumerate(pieces(m_all, 3)):
        pm_ref[pl.ds((npred + i) * levels, levels), :] = part

    cos_row = rows_ref[0:1, :]
    alb_row = rows_ref[1:2, :]
    day = (cos_row > 0.0).astype(f32)
    sub8 = lax.broadcasted_iota(jnp.int32, (SUBS, LANES), 0)
    day8 = jnp.zeros((SUBS, LANES), f32)
    for a in range(lane_rows):
        day8 = jnp.where(sub8 == a, day[:, a * LANES:(a + 1) * LANES], day8)
    r128 = lax.broadcasted_iota(jnp.int32, (LANES, LANES), 0)
    c128 = lax.broadcasted_iota(jnp.int32, (LANES, LANES), 1)
    tri = (r128 <= c128).astype(f32).astype(bf16)
    day8b = jnp.concatenate([day8, jnp.zeros_like(day8)], 0).astype(bf16)
    inner = dot(day8b, tri)[:SUBS]
    total = dot(day8b, jnp.ones((LANES, LANES), bf16))[:SUBS]
    before = jnp.zeros((SUBS, LANES), f32)
    for a in range(lane_rows - 1):
        before = before + jnp.where(sub8 > a, total[a:a + 1, :], 0.0)
    code = jnp.where(day8 > 0.5, inner + before, 0.0)
    n_day = jnp.sum(day8).astype(jnp.int32)
    for a in range(lane_rows):
        kk_ref[0:1, a * LANES:(a + 1) * LANES] = code[a:a + 1, :]
    high = jnp.floor(code * (1.0 / 32.0))
    low = code - 32.0 * high
    span = span_ref[...]
    slot = lax.div(span, cols) * per_peer + lax.rem(span, per_peer)
    pick_low = (
        (slot & (LANES - 1)) == lax.broadcasted_iota(jnp.int32, (LANES, cols), 0)
    ).astype(f32).astype(bf16)
    picked = dot(jnp.concatenate([high, low], 0).astype(bf16), pick_low)
    pick_high = (slot // LANES) == lax.broadcasted_iota(jnp.int32, (SUBS, cols), 0)
    merged = 32.0 * picked[:SUBS] + picked[SUBS:]
    kk_ref[1:2, :] = jnp.sum(jnp.where(pick_high, merged, 0.0), 0, keepdims=True)

    sub16 = lax.broadcasted_iota(jnp.int32, (16, cols), 0)
    ca = jnp.zeros((16, cols), f32)
    for i, part in enumerate(pieces(cos_row, 3) + pieces(alb_row, 3)):
        ca = jnp.where(sub16 == i, part.astype(f32), ca)
    ca_ref[...] = ca.astype(bf16)

    heat_ref[...] = jnp.zeros_like(heat_ref)
    surf_ref[...] = jnp.zeros_like(surf_ref)

    full = (n_day + 31) // LANES
    rem = jnp.maximum(n_day - full * LANES, 0)
    has64 = (rem > 32).astype(jnp.int32)
    has32 = (rem - 64 * has64 > 0).astype(jnp.int32)

    @pl.loop(0, full + has64 + has32)
    def chunk(c):
        is_full = c < full
        is_64 = jnp.logical_and(c == full, has64 == 1)
        width = jnp.where(is_full, LANES, jnp.where(is_64, LANES // 2, LANES // 4))
        base = jnp.where(
            is_full, c * LANES, full * LANES + jnp.where(is_64, 0, 64 * has64)
        )
        first = jnp.where(is_full, 0, jnp.where(is_64, 4, 6))
        count = jnp.where(is_full, 4, jnp.where(is_64, 2, 1))

        target = (
            base + 1 + (lax.broadcasted_iota(jnp.int32, (LANES, cols), 0) & (width - 1))
        ).astype(f32)
        ct_ref[...] = (kk_ref[0:1, :] == target).astype(f32).astype(bf16)
        mt_ref[...] = (kk_ref[1:2, :] == target).astype(f32).astype(bf16)
        comp_ref[...] = dot_t(pm_ref[...], mt_ref[...])
        column = lane & (width - 1)
        valid = base + column < n_day
        ca = dot_t(ca_ref[...], ct_ref[...])
        cosine = jnp.where(valid, ca[0:1] + ca[1:2] + ca[2:3], 1.0)
        albedo = ca[3:4] + ca[4:5] + ca[5:6]

        pack = lax.shift_right_logical(lane, jnp.where(is_full, 7, jnp.where(is_64, 6, 5)))
        m0 = npred * levels
        mh = jnp.where(valid, comp_ref[pl.ds(m0, levels), :], 1.0)
        mm = comp_ref[pl.ds(m0 + levels, levels), :]
        ml = comp_ref[pl.ds(m0 + 2 * levels, levels), :]
        mc_ref[...] = mh + mm + ml
        s16 = lax.broadcasted_iota(jnp.int32, (16, LANES), 0)

        def optics(r):
            for l in range(levels):
                optics_level(r, l)
            rows = g // r
            for l in range(0, levels, 2):
                two = sum(
                    dot(
                        wide_ref[q * rows:(q + 1) * rows, 0:section].astype(bf16),
                        rhs_ref[q * section:(q + 1) * section, l * LANES:(l + 2) * LANES],
                    )
                    for q in range(r)
                )
                tau_ref[l, 0:rows] = two[:, :LANES]
                tau_ref[l + 1, 0:rows] = two[:, LANES:]

        def optics_level(r, l):
            rr = jnp.where(s16 == 3, ml[l:l + 1], 0.0)
            rr = jnp.where((s16 == 1) | (s16 == 5), mm[l:l + 1], rr)
            rr = jnp.where((s16 == 0) | (s16 == 2) | (s16 == 4), mh[l:l + 1], rr)
            pred = comp_ref[pl.ds(l, npred, stride=levels), :]
            block = jnp.concatenate([pred, pred, rr], 0)
            for q in range(r):
                part = block if r == 1 else jnp.where(pack == q, block, 0.0)
                rhs_ref[q * section:(q + 1) * section, l * LANES:(l + 1) * LANES] = (
                    part.astype(bf16)
                )

        @pl.when(is_full)
        def _():
            optics(1)

        @pl.when(is_64)
        def _():
            optics(2)

        @pl.when(jnp.logical_not(jnp.logical_or(is_full, is_64)))
        def _():
            optics(4)

        net_ref[...] = jnp.zeros_like(net_ref)
        c_sun = 1.0 / (diffusivity * cosine)

        def fold(x):
            return jnp.sum(x.reshape(gb // SUBS, SUBS, LANES), 0)

        @pl.loop(0, count)
        def g_block(j):
            at = pl.multiple_of(j * gb, SUBS)
            table = pl.ds(pl.multiple_of((first + j) * gb, SUBS), gb)

            def up(i, carry):
                below_a, below_s = carry
                l = levels - 1 - i
                depth = tau_ref[l, pl.ds(at, gb), :]
                ray_m = ray_ref[table, :] * mc_ref[pl.ds(l, 1), :]
                half_w = ray_m * pl.reciprocal(depth, approx=True)
                ext = jnp.exp2(depth)
                sun = jnp.exp2(c_sun * depth)
                reflect = half_w - half_w * ext
                transmit = ext + reflect
                src = half_w - half_w * sun
                inv = pl.reciprocal(1.0 - reflect * below_a, approx=True)
                q = transmit * inv
                below_s_here = below_s * sun
                q_ref[l] = q
                v_ref[l] = (src + reflect * below_s_here) * inv
                e_ref[l] = sun
                a_ref[l] = below_a
                s_ref[l] = below_s
                next_a = reflect + (q * transmit) * below_a
                next_s = src + q * (below_s_here + below_a * src)
                return next_a, next_s

            start_a = jnp.broadcast_to(albedo, (gb, LANES))
            _, top_s = lax.fori_loop(0, levels, up, (start_a, start_a), unroll=8)

            direct = sol_ref[table, :] * cosine
            top_up = top_s * direct
            net_ref[0:SUBS, :] += fold(direct - top_up)

            def down(l, carry):
                diffuse, direct = carry
                diffuse = q_ref[l] * diffuse + direct * v_ref[l]
                direct = direct * e_ref[l]
                net = (direct + diffuse) - (a_ref[l] * diffuse + s_ref[l] * direct)
                rows = pl.ds(pl.multiple_of((l + 1) * SUBS, SUBS), SUBS)
                net_ref[rows, :] += fold(net)
                return diffuse, direct

            diffuse, direct = lax.fori_loop(
                0, levels, down, (jnp.zeros((gb, LANES), f32), direct), unroll=8
            )
            tail = (levels + 1) * SUBS
            net_ref[tail:tail + SUBS, :] += fold(direct)
            net_ref[tail + SUBS:tail + 2 * SUBS, :] += fold(diffuse)
            net_ref[tail + 2 * SUBS:tail + 3 * SUBS, :] += fold(top_up)

        upper = net_ref[pl.ds(0, levels, stride=SUBS), :]
        lower = net_ref[pl.ds(SUBS, levels, stride=SUBS), :]
        for s in range(1, SUBS):
            upper = upper + net_ref[pl.ds(s, levels, stride=SUBS), :]
            lower = lower + net_ref[pl.ds(SUBS + s, levels, stride=SUBS), :]
        heat = heat_factor * (upper - lower) / mc_ref[...]
        heat_ref[...] += sum(dot(part, mt_ref[...]) for part in pieces(heat, 2))
        tail = (levels + 1) * SUBS
        three = [
            jnp.sum(net_ref[tail + i * SUBS:tail + (i + 1) * SUBS, :], 0, keepdims=True)
            for i in range(3)
        ]
        surf8 = jnp.zeros((16, LANES), f32)
        for i in range(3):
            surf8 = jnp.where(s16 == i, three[i], surf8)
        surf_ref[...] += sum(dot(part, ct_ref[...]) for part in pieces(surf8, 2))[:SUBS]


def local(state, kdist, rayleigh, solar, span_map, cos_zenith, day_flag, albedo):
    fields, levels, columns = state.shape
    devices = lax.axis_size(("gx", "gy"))
    per_peer = columns // devices
    g, npred = kdist.shape
    gb = g // PACKS[-1]
    section = 2 * npred + 16
    local_rows = jnp.stack([cos_zenith, albedo])
    arrived = lax.all_to_all(local_rows, ("gx", "gy"), split_axis=1, concat_axis=1, tiled=True)
    vmem = pl.BlockSpec(memory_space=pltpu.VMEM)
    sweep = pltpu.VMEM((levels, gb, LANES), f32)
    heating, surface = pl.pallas_call(
        functools.partial(physics_kernel, per_peer),
        out_shape=(
            jax.ShapeDtypeStruct((levels, columns), f32),
            jax.ShapeDtypeStruct((SUBS, columns), f32),
        ),
        in_specs=[vmem] * 6,
        out_specs=(vmem, vmem),
        scratch_shapes=[
            pltpu.VMEM((LANES, -(-g // LANES) * LANES), f32),
            pltpu.VMEM((-(-g // LANES) * LANES, LANES), f32),
            pltpu.VMEM((gb * sum(PACKS), LANES), f32),
            pltpu.VMEM((gb * sum(PACKS), LANES), f32),
            pltpu.VMEM(((npred + 3) * levels, columns), bf16),
            pltpu.VMEM((16, columns), bf16),
            pltpu.VMEM((SUBS, columns), f32),
            pltpu.VMEM(((npred + 3) * levels, LANES), f32),
            pltpu.VMEM((levels, LANES), f32),
            pltpu.VMEM((PACKS[-1] * section, levels * LANES), bf16),
            pltpu.VMEM((LANES, columns), bf16),
            pltpu.VMEM((LANES, columns), bf16),
            pltpu.VMEM((levels, g, LANES), f32),
            sweep, sweep, sweep, sweep, sweep,
            pltpu.VMEM(((levels + 4) * SUBS, LANES), f32),
        ],
        compiler_params=pltpu.CompilerParams(vmem_limit_bytes=48 * 2**20),
    )(
        state, arrived, span_map.reshape(1, columns), kdist.T,
        rayleigh.reshape(1, g), solar.reshape(1, g),
    )
    surface = lax.all_to_all(surface[:3], ("gx", "gy"), split_axis=1, concat_axis=1, tiled=True)
    return (heating, surface)


def solution(mesh):
    in_specs = (
        P(None, None, ("gx", "gy")),
        P(),
        P(),
        P(),
        P(("gx", "gy")),
        P(("gx", "gy")),
        P(("gx", "gy")),
        P(("gx", "gy")),
    )
    out_specs = (P(None, ("gx", "gy")), P(None, ("gx", "gy")))
    return jax.shard_map(local, mesh=mesh, in_specs=in_specs, out_specs=out_specs, check_vma=False)
```

```python
import functools
import math

import jax
import jax.numpy as jnp
from jax import lax
from jax.experimental import pallas as pl
from jax.experimental.pallas import tpu as pltpu
from jax.sharding import PartitionSpec as P

diffusivity = 1.66
heat_factor = 8.0
LANES = 128
SUBS = 8
PACKS = (1, 2, 4)
LOG2E = math.log2(math.e)
f32 = jnp.float32
bf16 = jnp.bfloat16


def pieces(x, count):
    out = []
    for _ in range(count):
        part = x.astype(bf16)
        out.append(part)
        x = x - part.astype(f32)
    return out


def dot_t(a, b):
    return lax.dot_general(a, b, (((1,), (1,)), ((), ())), preferred_element_type=f32)


def dot(a, b):
    return jnp.dot(a, b, preferred_element_type=f32)


def physics_kernel(
    per_peer, state_hbm, span_hbm, kdist_hbm, gray_hbm, gsol_hbm, rows_ref,
    heat_ref, surf_ref,
    state_ref, span_ref, kdist_ref, gray_ref, gsol_ref, in_sem, basis_ref,
    tab_ref, wide_ref, ray_ref, sol_ref,
    pm_ref, ca_ref, kk_ref, comp_ref, mc_ref, rhs_ref, mt_ref, ct_ref,
    q_ref, v_ref, e_ref, a_ref, s_ref, net_ref,
):
    levels, cols = heat_ref.shape
    npred = 4 * (state_ref.shape[0] - 2)
    section = rhs_ref.shape[1] // PACKS[-1]
    fetch = [
        pltpu.make_async_copy(src, dst, in_sem.at[i])
        for i, (src, dst) in enumerate((
            (kdist_hbm, kdist_ref), (gray_hbm, gray_ref), (gsol_hbm, gsol_ref),
            (span_hbm, span_ref), (state_hbm, state_ref),
        ))
    ]
    for copy in fetch:
        copy.start()
    for copy in fetch[:4]:
        copy.wait()
    g = kdist_ref.shape[1]
    gb = g // PACKS[-1]
    c_diff = -diffusivity * LOG2E
    lane_rows = cols // LANES
    lane = lax.broadcasted_iota(jnp.int32, (1, LANES), 1)

    tab_ref[...] = jnp.zeros_like(tab_ref)
    kd = kdist_ref[...].astype(f32) * c_diff
    kd = jnp.concatenate(
        [kd[4 * i + b:4 * i + b + 1, :] for b in range(4) for i in range(npred // 4)], 0
    )
    high, low = pieces(kd, 2)
    tab_ref[0:npred, 0:g] = high.astype(f32)
    tab_ref[npred:2 * npred, 0:g] = low.astype(f32)
    gray = gray_ref[...]
    rh, rm, rl = [part.astype(f32) for part in pieces(gray * c_diff, 3)]
    sub16g = lax.broadcasted_iota(jnp.int32, (16, g), 0)
    tail16 = jnp.zeros((16, g), f32)
    for i, row in enumerate((rh, rh, rm, rh, rl, rm, gray * (0.5 * c_diff), gsol_ref[...])):
        tail16 = jnp.where(sub16g == i, row, tail16)
    tab_ref[2 * npred:2 * npred + 16, 0:g] = tail16
    turned = jnp.transpose(tab_ref[...])
    wide_ref[...] = turned
    for col, ref in ((2 * npred + 6, ray_ref), (2 * npred + 7, sol_ref)):
        spread = jnp.broadcast_to(turned[:g, col:col + 1], (g, LANES))
        at = 0
        for r in PACKS:
            rows = g // r
            value = spread[:rows]
            for q in range(1, r):
                value = jnp.where(lane >= q * (LANES // r), spread[q * rows:(q + 1) * rows], value)
            ref[at:at + rows, :] = value
            at += rows

    cos_row = rows_ref[0:1, :]
    alb_row = rows_ref[1:2, :]
    day = (cos_row > 0.0).astype(f32)
    sub8 = lax.broadcasted_iota(jnp.int32, (SUBS, LANES), 0)
    day8 = jnp.zeros((SUBS, LANES), f32)
    for a in range(lane_rows):
        day8 = jnp.where(sub8 == a, day[:, a * LANES:(a + 1) * LANES], day8)
    r128 = lax.broadcasted_iota(jnp.int32, (LANES, LANES), 0)
    c128 = lax.broadcasted_iota(jnp.int32, (LANES, LANES), 1)
    tri = (r128 <= c128).astype(f32).astype(bf16)
    day8b = jnp.concatenate([day8, jnp.zeros_like(day8)], 0).astype(bf16)
    inner = dot(day8b, tri)[:SUBS]
    total = dot(day8b, jnp.ones((LANES, LANES), bf16))[:SUBS]
    before = jnp.zeros((SUBS, LANES), f32)
    for a in range(lane_rows - 1):
        before = before + jnp.where(sub8 > a, total[a:a + 1, :], 0.0)
    code = jnp.where(day8 > 0.5, inner + before, 0.0)
    n_day = jnp.sum(day8).astype(jnp.int32)
    for a in range(lane_rows):
        kk_ref[0:1, a * LANES:(a + 1) * LANES] = code[a:a + 1, :]
    high = jnp.floor(code * (1.0 / 32.0))
    low = code - 32.0 * high
    span = span_ref[...]
    slot = lax.div(span, cols) * per_peer + lax.rem(span, per_peer)
    pick_low = (
        (slot & (LANES - 1)) == lax.broadcasted_iota(jnp.int32, (LANES, cols), 0)
    ).astype(f32).astype(bf16)
    picked = dot(jnp.concatenate([high, low], 0).astype(bf16), pick_low)
    pick_high = (slot // LANES) == lax.broadcasted_iota(jnp.int32, (SUBS, cols), 0)
    merged = 32.0 * picked[:SUBS] + picked[SUBS:]
    kk_ref[1:2, :] = jnp.sum(jnp.where(pick_high, merged, 0.0), 0, keepdims=True)

    sub16 = lax.broadcasted_iota(jnp.int32, (16, cols), 0)
    ca = jnp.zeros((16, cols), f32)
    for i, part in enumerate(pieces(cos_row, 3) + pieces(alb_row, 3)):
        ca = jnp.where(sub16 == i, part.astype(f32), ca)
    ca_ref[...] = ca.astype(bf16)

    fetch[4].wait()
    ngas = npred // 4
    t = state_ref[0] / 250.0
    basis_ref[0] = t
    basis_ref[1] = t * t
    basis_ref[2] = 1.0 / t
    m_all = state_ref[1]
    for i, part in enumerate(pieces(m_all, 3)):
        pm_ref[pl.ds((npred + i) * levels, levels), :] = part

    @pl.loop(0, levels, unroll=4)
    def level_predictors(l):
        gas = state_ref[2:2 + ngas, pl.ds(l, 1), :].reshape(ngas, cols)
        mass = state_ref[1, pl.ds(l, 1), :]
        values = [gas * mass]
        for b in range(3):
            values.append(gas * basis_ref[b, pl.ds(l, 1), :] * mass)
        rows = pl.ds(pl.multiple_of(l * npred, npred), npred)
        pm_ref[rows, :] = jnp.concatenate(values, 0).astype(bf16)

    heat_ref[...] = jnp.zeros_like(heat_ref)
    surf_ref[...] = jnp.zeros_like(surf_ref)

    full = (n_day + 31) // LANES
    rem = jnp.maximum(n_day - full * LANES, 0)
    has64 = (rem > 32).astype(jnp.int32)
    has32 = (rem - 64 * has64 > 0).astype(jnp.int32)

    s16 = lax.broadcasted_iota(jnp.int32, (16, LANES), 0)
    m0 = npred * levels
    c_gap = 1.0 / diffusivity

    def chunk(r, base):
        width = LANES // r
        rows = g // r
        first = gb * sum(PACKS[-1] // k for k in PACKS if k < r)
        target = (
            base + 1 + (lax.broadcasted_iota(jnp.int32, (LANES, cols), 0) & (width - 1))
        ).astype(f32)
        ct_ref[...] = (kk_ref[0:1, :] == target).astype(f32).astype(bf16)
        mt_ref[...] = (kk_ref[1:2, :] == target).astype(f32).astype(bf16)
        comp_ref[...] = dot_t(pm_ref[...], mt_ref[...])
        ca = dot_t(ca_ref[...], ct_ref[...])
        cosine = ca[0:1] + ca[1:2] + ca[2:3]
        albedo = ca[3:4] + ca[4:5] + ca[5:6]
        mh = comp_ref[m0:m0 + levels, :]
        valid = base + (lane & (width - 1)) < n_day
        cosine = jnp.where(valid, cosine, 1.0)
        mh = jnp.where(valid, mh, 1.0)
        comp_ref[m0:m0 + levels, :] = mh
        mc_ref[...] = (
            mh + comp_ref[m0 + levels:m0 + 2 * levels, :]
            + comp_ref[m0 + 2 * levels:m0 + 3 * levels, :]
        )
        pack = lane // width

        @pl.loop(0, levels, unroll=4)
        def right_side(l):
            ph, pm, plow = [comp_ref[pl.ds(m0 + i * levels + l, 1), :] for i in range(3)]
            rr = jnp.where(s16 == 3, plow, 0.0)
            rr = jnp.where((s16 == 1) | (s16 == 5), pm, rr)
            rr = jnp.where((s16 == 0) | (s16 == 2) | (s16 == 4), ph, rr)
            pred = comp_ref[pl.ds(pl.multiple_of(l * npred, npred), npred), :]
            for q in range(r):
                p, x = pred, rr
                if r > 1:
                    p = jnp.where(pack == q, p, 0.0)
                    x = jnp.where(pack == q, x, 0.0)
                p = p.astype(bf16)
                at = q * section
                rhs_ref[l, at:at + npred, :] = p
                rhs_ref[l, at + npred:at + 2 * npred, :] = p
                rhs_ref[l, at + 2 * npred:at + section, :] = x.astype(bf16)

        net_ref[...] = jnp.zeros_like(net_ref)
        c_sun = c_gap / cosine

        def fold(x):
            return jnp.sum(x.reshape(gb // SUBS, SUBS, LANES), 0)

        @pl.loop(0, PACKS[-1] // r)
        def g_block(j):
            table = pl.ds(pl.multiple_of(first + j * gb, SUBS), gb)
            lhs = [
                wide_ref[pl.ds(pl.multiple_of(q * rows + j * gb, SUBS), gb), 0:section].astype(bf16)
                for q in range(r)
            ]

            def up(i, carry):
                below_a, below_s = carry
                l = levels - 1 - i
                depth = sum(
                    dot(lhs[q], rhs_ref[l, q * section:(q + 1) * section, :]) for q in range(r)
                )
                ray_m = ray_ref[table, :] * mc_ref[pl.ds(l, 1), :]
                half_w = ray_m * pl.reciprocal(depth, approx=True)
                ext = jnp.exp2(depth)
                sun = jnp.exp2(c_sun * depth)
                reflect = half_w - half_w * ext
                transmit = ext + reflect
                src = half_w - half_w * sun
                inv = pl.reciprocal(1.0 - reflect * below_a, approx=True)
                q = transmit * inv
                below_s_here = below_s * sun
                q_ref[l] = q
                v_ref[l] = (src + reflect * below_s_here) * inv
                e_ref[l] = sun
                a_ref[l] = below_a
                s_ref[l] = below_s
                next_a = reflect + (q * transmit) * below_a
                next_s = src + q * (below_s_here + below_a * src)
                return next_a, next_s

            start_a = jnp.broadcast_to(albedo, (gb, LANES))
            _, top_s = lax.fori_loop(0, levels, up, (start_a, start_a), unroll=8)

            direct = sol_ref[table, :] * cosine
            top_up = top_s * direct
            net_ref[0:SUBS, :] += fold(direct - top_up)

            def down(l, carry):
                diffuse, direct = carry
                diffuse = q_ref[l] * diffuse + direct * v_ref[l]
                direct = direct * e_ref[l]
                net = (direct + diffuse) - (a_ref[l] * diffuse + s_ref[l] * direct)
                at = pl.ds(pl.multiple_of((l + 1) * SUBS, SUBS), SUBS)
                net_ref[at, :] += fold(net)
                return diffuse, direct

            diffuse, direct = lax.fori_loop(
                0, levels, down, (jnp.zeros((gb, LANES), f32), direct), unroll=8
            )
            tail = (levels + 1) * SUBS
            net_ref[tail:tail + SUBS, :] += fold(direct)
            net_ref[tail + SUBS:tail + 2 * SUBS, :] += fold(diffuse)
            net_ref[tail + 2 * SUBS:tail + 3 * SUBS, :] += fold(top_up)

        upper = net_ref[pl.ds(0, levels, stride=SUBS), :]
        lower = net_ref[pl.ds(SUBS, levels, stride=SUBS), :]
        for s in range(1, SUBS):
            upper = upper + net_ref[pl.ds(s, levels, stride=SUBS), :]
            lower = lower + net_ref[pl.ds(SUBS + s, levels, stride=SUBS), :]
        heat = heat_factor * (upper - lower) / mc_ref[...]
        heat_ref[...] += sum(dot(part, mt_ref[...]) for part in pieces(heat, 2))
        tail = (levels + 1) * SUBS
        three = [
            jnp.sum(net_ref[tail + i * SUBS:tail + (i + 1) * SUBS, :], 0, keepdims=True)
            for i in range(3)
        ]
        surf8 = jnp.zeros((16, LANES), f32)
        for i in range(3):
            surf8 = jnp.where(s16 == i, three[i], surf8)
        surf_ref[...] += sum(dot(part, ct_ref[...]) for part in pieces(surf8, 2))[:SUBS]

    @pl.loop(0, full)
    def whole_chunks(c):
        chunk(1, c * LANES)

    @pl.when(has64 == 1)
    def _():
        chunk(2, full * LANES)

    @pl.when(has32 == 1)
    def _():
        chunk(4, full * LANES + 64 * has64)


def exchange_kernel(rows, n, gy_size, *refs):
    count = (len(refs) - 6) // 2
    ins = refs[count + 1:2 * count + 1]
    out_ref = refs[count]
    send_ref, recv_ref, send_sem, recv_sem, in_sem = refs[2 * count + 1:]
    fetch = [
        pltpu.make_async_copy(refs[i], ins[i], in_sem.at[i]) for i in range(count)
    ]
    for copy in fetch:
        copy.start()
    cols = out_ref.shape[1]
    groups = cols // LANES
    share = cols // n
    per_group = LANES // share
    me = lax.axis_index("gx") * gy_size + lax.axis_index("gy")

    def device(d):
        return (lax.div(d, gy_size), lax.rem(d, gy_size))

    barrier = pltpu.get_barrier_semaphore()

    def greet(i, _):
        pl.semaphore_signal(
            barrier, inc=1, device_id=device(lax.rem(me + i, n)),
            device_id_type=pl.DeviceIdType.MESH,
        )
        return 0

    lax.fori_loop(1, n, greet, 0)
    send_ref[...] = jnp.zeros_like(send_ref)
    for copy in fetch:
        copy.wait()
    for a in range(groups):
        at = a * SUBS
        for ref in ins:
            count = min(ref.shape[0], rows)
            send_ref[at:at + count, :] = ref[0:count, a * LANES:(a + 1) * LANES]
            at += count
    pl.semaphore_wait(barrier, n - 1)

    def tile(i):
        return pl.ds(pl.multiple_of(i * SUBS, SUBS), SUBS)

    def outgoing(i):
        d = lax.rem(me + i, n)
        return pltpu.make_async_remote_copy(
            src_ref=send_ref.at[tile(lax.div(d, per_group))],
            dst_ref=recv_ref.at[tile(me)],
            send_sem=send_sem.at[i],
            recv_sem=recv_sem.at[i],
            device_id=device(d),
            device_id_type=pl.DeviceIdType.MESH,
        )

    def incoming(i):
        d = lax.rem(me + n - i, n)
        return pltpu.make_async_remote_copy(
            src_ref=recv_ref.at[tile(d)],
            dst_ref=recv_ref.at[tile(d)],
            send_sem=send_sem.at[i],
            recv_sem=recv_sem.at[i],
            device_id=device(d),
            device_id_type=pl.DeviceIdType.MESH,
        )

    def begin(i, _):
        outgoing(i).start()
        return 0

    def end(i, _):
        outgoing(i).wait_send()
        incoming(i).wait_recv()
        return 0

    lax.fori_loop(1, n, begin, 0)
    recv_ref[tile(me), :] = send_ref[tile(lax.div(me, per_group)), :]
    lax.fori_loop(1, n, end, 0)

    own = lax.rem(me, per_group) * share
    place = lax.broadcasted_iota(jnp.int32, (groups, LANES), 1) // share
    for r in range(rows):
        merged = jnp.zeros((groups, LANES), f32)
        for k in range(per_group):
            part = recv_ref[pl.ds(k * SUBS + r, groups, stride=SUBS * per_group), :]
            part = pltpu.roll(part, lax.rem(k * share + LANES - own, LANES), 1)
            merged = jnp.where(place == k, part, merged)
        for a in range(groups):
            out_ref[r:r + 1, a * LANES:(a + 1) * LANES] = merged[a:a + 1, :]


def exchange(inputs, rows, collective_id):
    n = lax.axis_size(("gx", "gy"))
    cols = inputs[0].shape[1]
    vmem = pl.BlockSpec(memory_space=pltpu.VMEM)
    return pl.pallas_call(
        functools.partial(exchange_kernel, rows, n, lax.axis_size("gy")),
        out_shape=jax.ShapeDtypeStruct((rows, cols), f32),
        in_specs=[pl.BlockSpec(memory_space=pltpu.HBM)] * len(inputs),
        out_specs=vmem,
        scratch_shapes=[pltpu.VMEM(x.shape, f32) for x in inputs] + [
            pltpu.VMEM((cols // LANES * SUBS, LANES), f32),
            pltpu.VMEM((n * SUBS, LANES), f32),
            pltpu.SemaphoreType.DMA((n,)),
            pltpu.SemaphoreType.DMA((n,)),
            pltpu.SemaphoreType.DMA((len(inputs),)),
        ],
        compiler_params=pltpu.CompilerParams(
            collective_id=collective_id, has_side_effects=True, vmem_limit_bytes=60 * 2**20
        ),
    )(*inputs)


def local(state, kdist, rayleigh, solar, span_map, cos_zenith, day_flag, albedo):
    fields, levels, columns = state.shape
    devices = lax.axis_size(("gx", "gy"))
    per_peer = columns // devices
    g, npred = kdist.shape
    gb = g // PACKS[-1]
    section = 2 * npred + 16
    arrived = exchange([cos_zenith.reshape(1, columns), albedo.reshape(1, columns)], 2, 0)
    vmem = pl.BlockSpec(memory_space=pltpu.VMEM)
    sweep = pltpu.VMEM((levels, gb, LANES), f32)
    heating, surface = pl.pallas_call(
        functools.partial(physics_kernel, per_peer),
        out_shape=(
            jax.ShapeDtypeStruct((levels, columns), f32),
            jax.ShapeDtypeStruct((SUBS, columns), f32),
        ),
        in_specs=[pl.BlockSpec(memory_space=pltpu.HBM)] * 5 + [vmem],
        out_specs=(vmem, vmem),
        scratch_shapes=[
            pltpu.VMEM(state.shape, f32),
            pltpu.VMEM((1, columns), jnp.int32),
            pltpu.VMEM((npred, g), bf16),
            pltpu.VMEM((1, g), f32),
            pltpu.VMEM((1, g), f32),
            pltpu.SemaphoreType.DMA((5,)),
            pltpu.VMEM((3, levels, columns), f32),
            pltpu.VMEM((LANES, -(-g // LANES) * LANES), f32),
            pltpu.VMEM((-(-g // LANES) * LANES, LANES), f32),
            pltpu.VMEM((gb * sum(PACKS), LANES), f32),
            pltpu.VMEM((gb * sum(PACKS), LANES), f32),
            pltpu.VMEM(((npred + 3) * levels, columns), bf16),
            pltpu.VMEM((16, columns), bf16),
            pltpu.VMEM((SUBS, columns), f32),
            pltpu.VMEM(((npred + 3) * levels, LANES), f32),
            pltpu.VMEM((levels, LANES), f32),
            pltpu.VMEM((levels, PACKS[-1] * section, LANES), bf16),
            pltpu.VMEM((LANES, columns), bf16),
            pltpu.VMEM((LANES, columns), bf16),
            sweep, sweep, sweep, sweep, sweep,
            pltpu.VMEM(((levels + 4) * SUBS, LANES), f32),
        ],
        compiler_params=pltpu.CompilerParams(vmem_limit_bytes=56 * 2**20),
    )(
        state, span_map.reshape(1, columns), kdist.T,
        rayleigh.reshape(1, g), solar.reshape(1, g), arrived,
    )
    surface = exchange([surface], 3, 1)
    return (heating, surface)


def solution(mesh):
    in_specs = (
        P(None, None, ("gx", "gy")),
        P(),
        P(),
        P(),
        P(("gx", "gy")),
        P(("gx", "gy")),
        P(("gx", "gy")),
        P(("gx", "gy")),
    )
    out_specs = (P(None, ("gx", "gy")), P(None, ("gx", "gy")))
    return jax.shard_map(local, mesh=mesh, in_specs=in_specs, out_specs=out_specs, check_vma=False)
```

```python
import functools
import math

import jax
import jax.numpy as jnp
from jax import lax
from jax.experimental import pallas as pl
from jax.experimental.pallas import tpu as pltpu
from jax.sharding import PartitionSpec as P

diffusivity = 1.66
heat_factor = 8.0
LANES = 128
SUBS = 8
PACKS = (1, 2, 4)
LOG2E = math.log2(math.e)
f32 = jnp.float32
bf16 = jnp.bfloat16


def pieces(x, count):
    out = []
    for _ in range(count):
        part = x.astype(bf16)
        out.append(part)
        x = x - part.astype(f32)
    return out


def dot_t(a, b):
    return lax.dot_general(a, b, (((1,), (1,)), ((), ())), preferred_element_type=f32)


def dot(a, b):
    return jnp.dot(a, b, preferred_element_type=f32)


def physics_kernel(
    per_peer, state_hbm, span_hbm, kdist_hbm, gray_hbm, gsol_hbm, rows_ref,
    heat_ref, surf_ref,
    state_ref, span_ref, kdist_ref, gray_ref, gsol_ref, in_sem, basis_ref,
    tab_ref, wide_ref, ray_ref, sol_ref,
    pm_ref, ca_ref, kk_ref, comp_ref, mc_ref, rhs_ref, mt_ref, ct_ref,
    tau_ref, q_ref, v_ref, e_ref, a_ref, s_ref, net_ref,
):
    levels, cols = heat_ref.shape
    npred = 4 * (state_ref.shape[0] - 2)
    section = rhs_ref.shape[1] // PACKS[-1]
    fetch = [
        pltpu.make_async_copy(src, dst, in_sem.at[i])
        for i, (src, dst) in enumerate((
            (kdist_hbm, kdist_ref), (gray_hbm, gray_ref), (gsol_hbm, gsol_ref),
            (span_hbm, span_ref), (state_hbm, state_ref),
        ))
    ]
    for copy in fetch:
        copy.start()
    for copy in fetch[:4]:
        copy.wait()
    g = kdist_ref.shape[1]
    gb = g // PACKS[-1]
    c_diff = -diffusivity * LOG2E
    lane_rows = cols // LANES
    lane = lax.broadcasted_iota(jnp.int32, (1, LANES), 1)

    tab_ref[...] = jnp.zeros_like(tab_ref)
    kd = kdist_ref[...].astype(f32) * c_diff
    kd = jnp.concatenate(
        [kd[4 * i + b:4 * i + b + 1, :] for b in range(4) for i in range(npred // 4)], 0
    )
    high, low = pieces(kd, 2)
    tab_ref[0:npred, 0:g] = high.astype(f32)
    tab_ref[npred:2 * npred, 0:g] = low.astype(f32)
    gray = gray_ref[...]
    rh, rm, rl = [part.astype(f32) for part in pieces(gray * c_diff, 3)]
    sub16g = lax.broadcasted_iota(jnp.int32, (16, g), 0)
    tail16 = jnp.zeros((16, g), f32)
    for i, row in enumerate((rh, rh, rm, rh, rl, rm, gray * (0.5 * c_diff), gsol_ref[...])):
        tail16 = jnp.where(sub16g == i, row, tail16)
    tab_ref[2 * npred:2 * npred + 16, 0:g] = tail16
    turned = jnp.transpose(tab_ref[...])
    wide_ref[...] = turned
    for col, ref in ((2 * npred + 6, ray_ref), (2 * npred + 7, sol_ref)):
        spread = jnp.broadcast_to(turned[:g, col:col + 1], (g, LANES))
        at = 0
        for r in PACKS:
            rows = g // r
            value = spread[:rows]
            for q in range(1, r):
                value = jnp.where(lane >= q * (LANES // r), spread[q * rows:(q + 1) * rows], value)
            ref[at:at + rows, :] = value
            at += rows

    cos_row = rows_ref[0:1, :]
    alb_row = rows_ref[1:2, :]
    day = (cos_row > 0.0).astype(f32)
    sub8 = lax.broadcasted_iota(jnp.int32, (SUBS, LANES), 0)
    day8 = jnp.zeros((SUBS, LANES), f32)
    for a in range(lane_rows):
        day8 = jnp.where(sub8 == a, day[:, a * LANES:(a + 1) * LANES], day8)
    r128 = lax.broadcasted_iota(jnp.int32, (LANES, LANES), 0)
    c128 = lax.broadcasted_iota(jnp.int32, (LANES, LANES), 1)
    tri = (r128 <= c128).astype(f32).astype(bf16)
    day8b = jnp.concatenate([day8, jnp.zeros_like(day8)], 0).astype(bf16)
    inner = dot(day8b, tri)[:SUBS]
    total = dot(day8b, jnp.ones((LANES, LANES), bf16))[:SUBS]
    before = jnp.zeros((SUBS, LANES), f32)
    for a in range(lane_rows - 1):
        before = before + jnp.where(sub8 > a, total[a:a + 1, :], 0.0)
    code = jnp.where(day8 > 0.5, inner + before, 0.0)
    n_day = jnp.sum(day8).astype(jnp.int32)
    for a in range(lane_rows):
        kk_ref[0:1, a * LANES:(a + 1) * LANES] = code[a:a + 1, :]
    high = jnp.floor(code * (1.0 / 32.0))
    low = code - 32.0 * high
    span = span_ref[...]
    slot = lax.div(span, cols) * per_peer + lax.rem(span, per_peer)
    pick_low = (
        (slot & (LANES - 1)) == lax.broadcasted_iota(jnp.int32, (LANES, cols), 0)
    ).astype(f32).astype(bf16)
    picked = dot(jnp.concatenate([high, low], 0).astype(bf16), pick_low)
    pick_high = (slot // LANES) == lax.broadcasted_iota(jnp.int32, (SUBS, cols), 0)
    merged = 32.0 * picked[:SUBS] + picked[SUBS:]
    kk_ref[1:2, :] = jnp.sum(jnp.where(pick_high, merged, 0.0), 0, keepdims=True)

    sub16 = lax.broadcasted_iota(jnp.int32, (16, cols), 0)
    ca = jnp.zeros((16, cols), f32)
    for i, part in enumerate(pieces(cos_row, 3) + pieces(alb_row, 3)):
        ca = jnp.where(sub16 == i, part.astype(f32), ca)
    ca_ref[...] = ca.astype(bf16)

    fetch[4].wait()
    ngas = npred // 4
    t = state_ref[0] / 250.0
    basis_ref[0] = t
    basis_ref[1] = t * t
    basis_ref[2] = 1.0 / t
    m_all = state_ref[1]
    for i, part in enumerate(pieces(m_all, 3)):
        pm_ref[pl.ds((npred + i) * levels, levels), :] = part

    @pl.loop(0, levels, unroll=4)
    def level_predictors(l):
        gas = state_ref[2:2 + ngas, pl.ds(l, 1), :].reshape(ngas, cols)
        mass = state_ref[1, pl.ds(l, 1), :]
        values = [gas * mass]
        for b in range(3):
            values.append(gas * basis_ref[b, pl.ds(l, 1), :] * mass)
        rows = pl.ds(pl.multiple_of(l * npred, npred), npred)
        pm_ref[rows, :] = jnp.concatenate(values, 0).astype(bf16)

    heat_ref[...] = jnp.zeros_like(heat_ref)
    surf_ref[...] = jnp.zeros_like(surf_ref)

    full = (n_day + 31) // LANES
    rem = jnp.maximum(n_day - full * LANES, 0)
    has64 = (rem > 32).astype(jnp.int32)
    has32 = (rem - 64 * has64 > 0).astype(jnp.int32)

    s16 = lax.broadcasted_iota(jnp.int32, (16, LANES), 0)
    m0 = npred * levels
    c_gap = 1.0 / diffusivity

    def chunk(r, base):
        width = LANES // r
        rows = g // r
        first = gb * sum(PACKS[-1] // k for k in PACKS if k < r)
        target = (
            base + 1 + (lax.broadcasted_iota(jnp.int32, (LANES, cols), 0) & (width - 1))
        ).astype(f32)
        ct_ref[...] = (kk_ref[0:1, :] == target).astype(f32).astype(bf16)
        mt_ref[...] = (kk_ref[1:2, :] == target).astype(f32).astype(bf16)
        comp_ref[...] = dot_t(pm_ref[...], mt_ref[...])
        ca = dot_t(ca_ref[...], ct_ref[...])
        cosine = ca[0:1] + ca[1:2] + ca[2:3]
        albedo = ca[3:4] + ca[4:5] + ca[5:6]
        mh = comp_ref[m0:m0 + levels, :]
        valid = base + (lane & (width - 1)) < n_day
        cosine = jnp.where(valid, cosine, 1.0)
        mh = jnp.where(valid, mh, 1.0)
        comp_ref[m0:m0 + levels, :] = mh
        mc_ref[...] = (
            mh + comp_ref[m0 + levels:m0 + 2 * levels, :]
            + comp_ref[m0 + 2 * levels:m0 + 3 * levels, :]
        )
        pack = lane // width

        lhs = [
            wide_ref[q * rows:(q + 1) * rows, 0:section].astype(bf16) for q in range(r)
        ]

        def right_side(pair, half):
            l = 2 * pair + half
            ph, pm, plow = [comp_ref[pl.ds(m0 + i * levels + l, 1), :] for i in range(3)]
            rr = jnp.where(s16 == 3, plow, 0.0)
            rr = jnp.where((s16 == 1) | (s16 == 5), pm, rr)
            rr = jnp.where((s16 == 0) | (s16 == 2) | (s16 == 4), ph, rr)
            pred = comp_ref[pl.ds(pl.multiple_of(l * npred, npred), npred), :]
            lanes = slice(half * LANES, (half + 1) * LANES)
            for q in range(r):
                p, x = pred, rr
                if r > 1:
                    p = jnp.where(pack == q, p, 0.0)
                    x = jnp.where(pack == q, x, 0.0)
                p = p.astype(bf16)
                at = q * section
                rhs_ref[pair, at:at + npred, lanes] = p
                rhs_ref[pair, at + npred:at + 2 * npred, lanes] = p
                rhs_ref[pair, at + 2 * npred:at + section, lanes] = x.astype(bf16)

        @pl.loop(0, levels // 2, unroll=4)
        def optics(pair):
            right_side(pair, 0)
            right_side(pair, 1)

        @pl.loop(0, levels // 2, unroll=4)
        def depths(pair):
            two = sum(
                dot(lhs[q], rhs_ref[pair, q * section:(q + 1) * section, :]) for q in range(r)
            )
            tau_ref[2 * pair, 0:rows] = two[:, :LANES]
            tau_ref[2 * pair + 1, 0:rows] = two[:, LANES:]

        net_ref[...] = jnp.zeros_like(net_ref)
        c_sun = c_gap / cosine

        def fold(x):
            return jnp.sum(x.reshape(gb // SUBS, SUBS, LANES), 0)

        @pl.loop(0, PACKS[-1] // r)
        def g_block(j):
            table = pl.ds(pl.multiple_of(first + j * gb, SUBS), gb)
            own = pl.ds(pl.multiple_of(j * gb, SUBS), gb)

            def up(i, carry):
                below_a, below_s = carry
                l = levels - 1 - i
                depth = tau_ref[l, own, :]
                ray_m = ray_ref[table, :] * mc_ref[pl.ds(l, 1), :]
                half_w = ray_m * pl.reciprocal(depth, approx=True)
                ext = jnp.exp2(depth)
                sun = jnp.exp2(c_sun * depth)
                reflect = half_w - half_w * ext
                transmit = ext + reflect
                src = half_w - half_w * sun
                inv = pl.reciprocal(1.0 - reflect * below_a, approx=True)
                q = transmit * inv
                below_s_here = below_s * sun
                q_ref[l] = q
                v_ref[l] = (src + reflect * below_s_here) * inv
                e_ref[l] = sun
                a_ref[l] = below_a
                s_ref[l] = below_s
                next_a = reflect + (q * transmit) * below_a
                next_s = src + q * (below_s_here + below_a * src)
                return next_a, next_s

            start_a = jnp.broadcast_to(albedo, (gb, LANES))
            _, top_s = lax.fori_loop(0, levels, up, (start_a, start_a), unroll=16)

            direct = sol_ref[table, :] * cosine
            top_up = top_s * direct
            net_ref[0:SUBS, :] += fold(direct - top_up)

            def down(l, carry):
                diffuse, direct = carry
                diffuse = q_ref[l] * diffuse + direct * v_ref[l]
                direct = direct * e_ref[l]
                net = (direct + diffuse) - (a_ref[l] * diffuse + s_ref[l] * direct)
                at = pl.ds(pl.multiple_of((l + 1) * SUBS, SUBS), SUBS)
                net_ref[at, :] += fold(net)
                return diffuse, direct

            diffuse, direct = lax.fori_loop(
                0, levels, down, (jnp.zeros((gb, LANES), f32), direct), unroll=16
            )
            tail = (levels + 1) * SUBS
            net_ref[tail:tail + SUBS, :] += fold(direct)
            net_ref[tail + SUBS:tail + 2 * SUBS, :] += fold(diffuse)
            net_ref[tail + 2 * SUBS:tail + 3 * SUBS, :] += fold(top_up)

        upper = net_ref[pl.ds(0, levels, stride=SUBS), :]
        lower = net_ref[pl.ds(SUBS, levels, stride=SUBS), :]
        for s in range(1, SUBS):
            upper = upper + net_ref[pl.ds(s, levels, stride=SUBS), :]
            lower = lower + net_ref[pl.ds(SUBS + s, levels, stride=SUBS), :]
        heat = heat_factor * (upper - lower) / mc_ref[...]
        heat_ref[...] += sum(dot(part, mt_ref[...]) for part in pieces(heat, 2))
        tail = (levels + 1) * SUBS
        three = [
            jnp.sum(net_ref[tail + i * SUBS:tail + (i + 1) * SUBS, :], 0, keepdims=True)
            for i in range(3)
        ]
        surf8 = jnp.zeros((16, LANES), f32)
        for i in range(3):
            surf8 = jnp.where(s16 == i, three[i], surf8)
        surf_ref[...] += sum(dot(part, ct_ref[...]) for part in pieces(surf8, 2))[:SUBS]

    @pl.loop(0, full)
    def whole_chunks(c):
        chunk(1, c * LANES)

    @pl.when(has64 == 1)
    def _():
        chunk(2, full * LANES)

    @pl.when(has32 == 1)
    def _():
        chunk(4, full * LANES + 64 * has64)


def local(state, kdist, rayleigh, solar, span_map, cos_zenith, day_flag, albedo):
    fields, levels, columns = state.shape
    devices = lax.axis_size(("gx", "gy"))
    per_peer = columns // devices
    g, npred = kdist.shape
    gb = g // PACKS[-1]
    section = 2 * npred + 16
    arrived = lax.all_to_all(
        jnp.stack([cos_zenith, albedo]), ("gx", "gy"), split_axis=1, concat_axis=1, tiled=True
    )
    vmem = pl.BlockSpec(memory_space=pltpu.VMEM)
    sweep = pltpu.VMEM((levels, gb, LANES), f32)
    heating, surface = pl.pallas_call(
        functools.partial(physics_kernel, per_peer),
        out_shape=(
            jax.ShapeDtypeStruct((levels, columns), f32),
            jax.ShapeDtypeStruct((SUBS, columns), f32),
        ),
        in_specs=[pl.BlockSpec(memory_space=pltpu.HBM)] * 5 + [vmem],
        out_specs=(vmem, vmem),
        scratch_shapes=[
            pltpu.VMEM(state.shape, f32),
            pltpu.VMEM((1, columns), jnp.int32),
            pltpu.VMEM((npred, g), bf16),
            pltpu.VMEM((1, g), f32),
            pltpu.VMEM((1, g), f32),
            pltpu.SemaphoreType.DMA((5,)),
            pltpu.VMEM((3, levels, columns), f32),
            pltpu.VMEM((LANES, -(-g // LANES) * LANES), f32),
            pltpu.VMEM((-(-g // LANES) * LANES, LANES), f32),
            pltpu.VMEM((gb * sum(PACKS), LANES), f32),
            pltpu.VMEM((gb * sum(PACKS), LANES), f32),
            pltpu.VMEM(((npred + 3) * levels, columns), bf16),
            pltpu.VMEM((16, columns), bf16),
            pltpu.VMEM((SUBS, columns), f32),
            pltpu.VMEM(((npred + 3) * levels, LANES), f32),
            pltpu.VMEM((levels, LANES), f32),
            pltpu.VMEM((levels // 2, PACKS[-1] * section, 2 * LANES), bf16),
            pltpu.VMEM((LANES, columns), bf16),
            pltpu.VMEM((LANES, columns), bf16),
            pltpu.VMEM((levels, g, LANES), f32),
            sweep, sweep, sweep, sweep, sweep,
            pltpu.VMEM(((levels + 4) * SUBS, LANES), f32),
        ],
        compiler_params=pltpu.CompilerParams(vmem_limit_bytes=56 * 2**20),
    )(
        state, span_map.reshape(1, columns), kdist.T,
        rayleigh.reshape(1, g), solar.reshape(1, g), arrived,
    )
    surface = lax.all_to_all(surface[:3], ("gx", "gy"), split_axis=1, concat_axis=1, tiled=True)
    return (heating, surface)


def solution(mesh):
    in_specs = (
        P(None, None, ("gx", "gy")),
        P(),
        P(),
        P(),
        P(("gx", "gy")),
        P(("gx", "gy")),
        P(("gx", "gy")),
        P(("gx", "gy")),
    )
    out_specs = (P(None, ("gx", "gy")), P(None, ("gx", "gy")))
    return jax.shard_map(local, mesh=mesh, in_specs=in_specs, out_specs=out_specs, check_vma=False)
```
